32 devices in a mesh: grp: 2 (over y), col: 4 (over x, core), row: 4 (over z).
Axes of the slice: x: 2, y: 2, z: 4, core: 2. Of those that a mesh axis runs over, the one named last changes fastest.
Arguments:
- tokens: bfloat16 [1024, 7168], P(('grp', 'col'), 'row'), parts along dimension 0, may hold values from -6 to 6
- expert_ids: int32 [1024, 8], P(('grp', 'col')), parts along dimension 0, may hold values from 0 to 15, all different within a row; in each aligned block of 128 rows (0 to 127, 128 to 255, ...) at most 80 rows name the same one
- weight_index: int32 [1024, 8], P(('grp', 'col')), parts along dimension 0, may hold values from 0 to 63
- combine_table: float32 [64], replicated, may hold values from 0.1 to 1
- gate_weight: bfloat16 [16, 7168, 2048], P('col', None, 'row'), may hold values from -0.0625 to 0.0625
- up_weight: bfloat16 [16, 7168, 2048], P('col', None, 'row'), may hold values from -0.0625 to 0.0625
- down_weight: bfloat16 [16, 2048, 7168], P('col', None, 'row'), may hold values from -0.125 to 0.125
Outputs:
- layer_output: bfloat16 [1024, 7168], P(('grp', 'col'), 'row'), parts along dimension 0
The draws below stay inside these ranges and needn't reach their ends.
There are 2 independent parts, one for each index of `grp`. The reference program is written for one: setup_inputs(seed, part) draws one part's arguments, and reference() takes and returns one part's arrays. A program takes and returns all parts, laid end to end along the dimension named above; an argument that names none is the same for every part. Nothing has to cross between parts.
Inputs may be any that keep to these rules, and one draw needn't show every extreme that they name: `expert_ids`: each row names 8 different experts, and every expert is named somewhere. Within the 128 rows of one index of col (aligned blocks), no expert is named by more than 80 rows.
All inputs are finite; a program needn't handle non-finite values.
Results may differ from the reference program's by a relative error of at most 0.0057.
Values may be sent and summed in bfloat16 or wider, within the bound.
A program may use at most 192 MiB of HBM per device.

```python
import math
from functools import partial
import jax
import jax.numpy as jnp
import numpy as np
from jax import lax

D = 7168
FF = 2048
TOP = 8
EXPERTS = 16
TABLE = 64
TOK_DEV = 128
CAP = 80
TOKENS = 512


def with_ends(result, key, least, high):
    place = [jax.random.randint(jax.random.fold_in(key, axis), (), 0, length) for axis, length in enumerate(result.shape)]
    longest = result.shape.index(max(result.shape))
    neighbour = place[:longest] + [(place[longest] + 1) % result.shape[longest]] + place[longest + 1:]
    return result.at[tuple(place)].set(least).at[tuple(neighbour)].set(high)


def block_levels(key, dims, pieces, smallest, top_value):
    gain = 1.0
    for position, blocks in pieces:
        steps = jax.random.uniform(jax.random.fold_in(jax.random.fold_in(key, 6), position), (blocks,), jnp.float32, smallest / len(pieces), top_value / len(pieces))
        gain = gain * jnp.repeat(jnp.exp(steps), dims[position] // blocks).reshape((-1,) + (1,) * (len(dims) - 1 - position))
    return gain


def routed_block(stream_key, own, number, rows, amount, top, most, slope):
    order = jax.random.permutation(stream_key, amount)
    packed, common = load_shares(amount, rows * top, most, slope, True), load_shares(amount, rows * top, most, slope, False)
    places = jnp.arange(amount)

    def named(sizes, turn):
        used = int((sizes > 0).sum())
        fixed = max(1, used // 4)
        moved = fixed + (places - fixed + turn * (used - fixed)) % max(1, amount - fixed)
        return jnp.zeros((amount,), jnp.int32).at[order[jnp.where(places < fixed, places, moved)]].set(jnp.asarray(sizes, jnp.int32))

    sizes = jnp.where(number % 4 == 0, named(packed, number // 4), named(common, number - number // 4 - 1))
    mixed = jax.random.permutation(jax.random.fold_in(own, 3), amount)
    giver, receiver = mixed[0:amount // 2 * 2:2], mixed[1:amount // 2 * 2:2]
    margin = jnp.minimum(sizes[giver] - 1, most - sizes[receiver]) // 2
    margin = jnp.where((giver == order[0]) | (receiver == order[0]) | (sizes[receiver] == 0), 0, jnp.maximum(margin, 0))
    moved = jax.random.randint(jax.random.fold_in(own, 4), (amount // 2,), 0, 1 << 20) % (margin + 1)
    sizes = sizes.at[giver].add(-moved).at[receiver].add(moved)
    members = jnp.searchsorted(jnp.cumsum(sizes), jnp.arange(rows * top), side="right").astype(jnp.int32)
    grid = members.reshape(top, rows).T
    grid = grid[jax.random.permutation(jax.random.fold_in(own, 1), rows)]
    turn = jax.random.randint(jax.random.fold_in(own, 2), (rows, 1), 0, top)
    return jnp.take_along_axis(grid, (jnp.arange(top)[None, :] + turn) % top, axis=1)


def load_shares(amount, total, limit, skew, full):
    portions = [(1 << 20) // math.isqrt(rank ** skew) + 1 for rank in range(1, amount + 1)]
    largest = limit if full else min(limit, max(-(-total // amount), total * portions[0] // sum(portions)))
    least = 1 if total - largest >= amount - 1 else 0
    counts, surplus = [largest] + [least] * (amount - 1), total - largest - least * (amount - 1)
    while surplus > 0:
        free = [i for i in range(1, amount) if counts[i] < largest] or [i for i in range(1, amount) if counts[i] < limit]
        whole, remaining = sum([portions[i] for i in free]), surplus
        for i in free:
            extra = min(limit - counts[i], max(1, remaining * portions[i] // whole), surplus)
            counts[i] = counts[i] + extra
            surplus = surplus - extra
    return np.array(counts)


def noise(key, dims, deviation, most, cuts=(), kind=jnp.bfloat16):
    array = jax.random.normal(key, dims, jnp.float32) * deviation
    if len(cuts) > 0:
        array = block_levels(key, dims, cuts, -0.22, 0.18) * array
    return jnp.clip(array, min=-most, max=most).astype(kind)


def setup_inputs(seed: int = 0, part: int = 0) -> dict:
    keys = jax.random.split(jax.random.key(seed), 8)
    part_splits = jax.random.split(jax.random.fold_in(keys[7], part), 8)
    tokens = noise(part_splits[0], (TOKENS, D), 1.0, 6.0, ((0, 4), (1, 4)))
    expert_ids_keys = jax.random.split(jax.random.fold_in(part_splits[1], 1), TOKENS // TOK_DEV)
    expert_ids_turns = jax.random.permutation(jax.random.fold_in(part_splits[1], 3), TOKENS // TOK_DEV)
    expert_ids = jax.vmap(lambda own, number: routed_block(jax.random.fold_in(part_splits[1], 2), own, number, TOK_DEV, EXPERTS, TOP, CAP, 2))(expert_ids_keys, expert_ids_turns).reshape((TOKENS, TOP))
    weight_index = with_ends(jax.random.randint(part_splits[2], (TOKENS, TOP), 0, TABLE), jax.random.fold_in(part_splits[2], 1), 0, TABLE - 1).astype(jnp.int32)
    combine_table = jnp.clip(jnp.exp(jax.random.uniform(keys[3], (TABLE,), jnp.float32, math.log(0.1), math.log(1.0))), 0.1, 1.0)
    gate_weight = noise(keys[4], (EXPERTS, D, FF), D ** -0.5, 0.0625, ((0, 4), (2, 4)))
    up_weight = noise(keys[5], (EXPERTS, D, FF), D ** -0.5, 0.0625, ((0, 4), (2, 4)))
    down_weight = noise(keys[6], (EXPERTS, FF, D), FF ** -0.5, 0.125, ((0, 4), (2, 4)))
    return dict(tokens=tokens, expert_ids=expert_ids, weight_index=weight_index, combine_table=combine_table, gate_weight=gate_weight, up_weight=up_weight, down_weight=down_weight)


route_scale = 2.827


def slot_table(picked_ids, experts, capacity):
    count, picks = picked_ids.shape
    flat_ids = picked_ids.reshape(-1).astype(jnp.int32)
    one_hot = (flat_ids[:, None] == jnp.arange(experts, dtype=jnp.int32)[None, :]).astype(jnp.int32)
    ranking = jnp.sum((jnp.cumsum(one_hot, axis=0) - 1) * one_hot, axis=1).astype(jnp.int32)
    placing = (flat_ids * capacity + ranking).astype(jnp.int32)
    entries = (jnp.arange(count * picks, dtype=jnp.int32) // picks).astype(jnp.int32)
    holder = jnp.full((experts * capacity,), -1, jnp.int32).at[placing].set(entries)
    return holder, placing


def combine_weights(weight_index, combine_table):
    table_size = combine_table.shape[0]
    match = weight_index[..., None] == jnp.arange(table_size, dtype=jnp.int32)
    table_values = jnp.sum(jnp.where(match, combine_table.astype(jnp.float32), jnp.float32(0.0)), axis=-1)
    return route_scale * table_values / jnp.sum(table_values, axis=-1, keepdims=True)


def reference(tokens, expert_ids, weight_index, combine_table, gate_weight, up_weight, down_weight):
    groups = TOKENS // TOK_DEV
    block_ids = expert_ids.reshape(groups, TOK_DEV, TOP)
    holder, placing = jax.vmap(partial(slot_table, experts=EXPERTS, capacity=CAP))(block_ids)
    offsets = (jnp.arange(groups, dtype=jnp.int32) * TOK_DEV)[:, None]
    global_holder = jnp.where(holder >= 0, holder + offsets, -1).astype(jnp.int32)
    slot_lists = global_holder.reshape(groups, EXPERTS, CAP).transpose(1, 0, 2).reshape(EXPERTS, groups * CAP)

    def expert(operands):
        slot_index, gate_mat, up_mat, down_mat = operands
        is_valid = slot_index >= 0
        routed_rows = jnp.take(tokens, jnp.maximum(slot_index, 0), axis=0)
        routed_rows = jnp.where(is_valid[:, None], routed_rows, jnp.zeros((), tokens.dtype))
        gate_part = jnp.dot(routed_rows, gate_mat, preferred_element_type=jnp.float32)
        up_part = jnp.dot(routed_rows, up_mat, preferred_element_type=jnp.float32)
        hidden = (jax.nn.silu(gate_part) * up_part).astype(jnp.bfloat16)
        return jnp.dot(hidden, down_mat, preferred_element_type=jnp.float32).astype(jnp.bfloat16)

    expert_out = lax.map(expert, (slot_lists, gate_weight, up_weight, down_weight))
    group_base = (jnp.arange(groups, dtype=jnp.int32) * CAP)[:, None]
    found = ((placing // CAP) * (groups * CAP) + group_base + placing % CAP).astype(jnp.int32)
    gathered = jnp.take(expert_out.reshape(EXPERTS * groups * CAP, D), found.reshape(-1), axis=0)
    gathered = gathered.reshape(TOKENS, TOP, D).astype(jnp.float32)
    weights = combine_weights(weight_index, combine_table)
    return jnp.sum(weights[..., None] * gathered, axis=1).astype(jnp.bfloat16)
```

```python
import functools

import jax
import jax.numpy as jnp
from jax import lax
from jax.experimental import pallas as pl
from jax.experimental.pallas import tpu as pltpu
from jax.sharding import PartitionSpec as P

CAP = 80


route_scale = 2.827


def slot_table(picked_ids, experts, capacity):
    count, picks = picked_ids.shape
    flat_ids = picked_ids.reshape(-1)
    one_hot = (flat_ids[:, None] == jnp.arange(experts, dtype=jnp.int32)[None, :]).astype(jnp.int32)
    ranking = jnp.sum((jnp.cumsum(one_hot, axis=0) - 1) * one_hot, axis=1)
    placing = flat_ids * capacity + ranking
    entries = jnp.arange(count * picks, dtype=jnp.int32) // picks
    holder = jnp.full((experts * capacity,), -1, jnp.int32).at[placing].set(entries)
    return (holder, placing)


def combine_weights(weight_index, combine_table):
    table_size = combine_table.shape[0]
    match = weight_index[..., None] == jnp.arange(table_size, dtype=jnp.int32)
    table_values = jnp.sum(jnp.where(match, combine_table, jnp.float32(0.0)), axis=-1)
    return route_scale * table_values / jnp.sum(table_values, axis=-1, keepdims=True)


def select_rows(source, holder, col_count, local_experts):
    is_valid = holder >= 0
    picked = jnp.take(source, jnp.maximum(holder, 0), axis=0)
    picked = jnp.where(is_valid[:, None], picked, jnp.zeros((), source.dtype))
    return picked.reshape(col_count, local_experts, CAP, source.shape[1])


def plain_shards(tokens, expert_ids, weight_index, combine_table, gate_weight, up_weight, down_weight):
    col_count = lax.axis_size("col")
    local_experts = gate_weight.shape[0]
    experts = local_experts * col_count
    holder, placing = slot_table(expert_ids, experts, CAP)
    full_tokens = lax.all_gather(tokens, "row", axis=1, tiled=True)
    outgoing = select_rows(full_tokens, holder, col_count, local_experts)
    arrived = lax.all_to_all(outgoing, "col", split_axis=0, concat_axis=0, tiled=True)
    gate_part = jnp.einsum(
        "secw,ewf->secf", arrived, gate_weight, preferred_element_type=jnp.float32
    )
    up_part = jnp.einsum("secw,ewf->secf", arrived, up_weight, preferred_element_type=jnp.float32)
    hidden = (jax.nn.silu(gate_part) * up_part).astype(jnp.bfloat16)
    expert_out = jnp.einsum(
        "secf,efd->secd",
        lax.all_gather(hidden, "row", axis=3, tiled=True),
        down_weight,
        preferred_element_type=jnp.float32,
    ).astype(jnp.bfloat16)
    returned = lax.all_to_all(expert_out, "col", split_axis=0, concat_axis=0, tiled=True)
    features = returned.shape[3]
    gathered = jnp.take(returned.reshape(experts * CAP, features), placing, axis=0)
    gathered = gathered.reshape(expert_ids.shape + (features,)).astype(jnp.float32)
    weights = combine_weights(weight_index, combine_table)
    return jnp.sum(weights[..., None] * gathered, axis=1).astype(jnp.bfloat16)


TILE = 256
VMEM_BYTES = 60 * 1024 * 1024
MESH = pl.DeviceIdType.MESH


def expert_kernel(
    geometry, tok_hbm, meta_ref, table_ref, gate_hbm, up_hbm, down_hbm, out_ref,
    tok_all, meta_all, gate_buf, up_buf, down_buf, acc_gate, acc_up, place, spread, slot_weight,
    hid, acc, part, sib_in, x_out, x_in,
    local_sem, gate_sem, up_sem, down_sem, meta_send, meta_recv, tok_send, tok_recv,
    hid_send, hid_recv, part_send, part_recv,
):
    cols, rows, count, picks, local, width, hidden, table = geometry
    slots = cols * CAP
    chunks = hidden // TILE
    g = lax.axis_index("grp")
    c = lax.axis_index("col")
    r = lax.axis_index("row")
    core, chip = c % 2, c // 2
    col_of = [c, 2 * chip + 1 - core, 2 * (1 - chip) + core, 2 * (1 - chip) + 1 - core]
    has_up, has_down = r < rows - 1, r > 0

    def remote(src, dst, send, recv, col, row):
        return pltpu.make_async_remote_copy(
            src_ref=src, dst_ref=dst, send_sem=send, recv_sem=recv,
            device_id=(g, col, row), device_id_type=MESH,
        )

    def block(q, s):
        return tok_all.at[q, pl.ds(pl.multiple_of(s * count, count), count), :]

    def tok_copy(kind, q):
        s = col_of[2] if kind == 4 else c
        col = (c, c, col_of[1], col_of[2], col_of[1])[kind]
        row = (r + 1, r - 1, r, r, r)[kind]
        relation = (0, 0, 1, 2, 3)[kind]
        return remote(block(q, s), block(q, s), tok_send.at[kind, q], tok_recv.at[relation, q], col, row)

    def tok_wait(relation, q):
        view = block(q, col_of[relation])
        remote(view, view, tok_send.at[0, q], tok_recv.at[relation, q], c, r).wait_recv()

    def hid_copy(direction, e, q):
        view = hid.at[e, q]
        return remote(
            view, view, hid_send.at[direction, e, q], hid_recv.at[e, q], c, (r + 1, r - 1)[direction]
        )

    def weight_copies(e, n):
        cut = pl.ds(pl.multiple_of(n * TILE, TILE), TILE)
        return (
            pltpu.make_async_copy(gate_hbm.at[e, :, cut], gate_buf.at[n], gate_sem.at[n]),
            pltpu.make_async_copy(up_hbm.at[e, :, cut], up_buf.at[n], up_sem.at[n]),
        )

    def down_copy(e, slot):
        return pltpu.make_async_copy(down_hbm.at[e], down_buf.at[slot], down_sem.at[slot])

    local_copy = pltpu.make_async_copy(tok_hbm, block(r, c), local_sem)
    local_copy.start()
    for n in range(chunks):
        for copy in weight_copies(0, n):
            copy.start()
    for e in range(min(2, local)):
        down_copy(e, e).start()

    barrier = pltpu.get_barrier_semaphore()
    for k in (1, 2, 3):
        pl.semaphore_signal(barrier, inc=1, device_id=(g, col_of[k], r), device_id_type=MESH)

    @pl.when(has_up)
    def _():
        pl.semaphore_signal(barrier, inc=1, device_id=(g, c, r + 1), device_id_type=MESH)

    @pl.when(has_down)
    def _():
        pl.semaphore_signal(barrier, inc=1, device_id=(g, c, r - 1), device_id_type=MESH)

    pl.semaphore_wait(barrier, 3 + jnp.where(has_up, 1, 0) + jnp.where(has_down, 1, 0))

    def meta_copy(k):
        return remote(meta_ref, meta_all.at[c], meta_send.at[k - 1], meta_recv.at[k - 1], col_of[k], r)

    for k in (1, 2, 3):
        meta_copy(k).start()
    local_copy.wait()

    def spread_tokens(q, upward, downward):
        @pl.when(upward)
        def _():
            tok_copy(0, q).start()

        @pl.when(downward)
        def _():
            tok_copy(1, q).start()

        tok_copy(3, q).start()
        tok_copy(2, q).start()

    spread_tokens(r, has_up, has_down)

    meta_all[c] = meta_ref[...]
    acc[...] = jnp.zeros_like(acc)
    for k in (1, 2, 3):
        view = meta_all.at[col_of[k]]
        remote(meta_ref, view, meta_send.at[k - 1], meta_recv.at[k - 1], c, r).wait_recv()
    before = (
        lax.broadcasted_iota(jnp.int32, (count, count), 0)
        < lax.broadcasted_iota(jnp.int32, (count, count), 1)
    ).astype(jnp.float32).astype(jnp.bfloat16)
    line = lax.broadcasted_iota(jnp.int32, (count, count), 0).astype(jnp.float32)

    @pl.loop(0, cols)
    def _(s):
        ids = meta_all[s, 0:picks, :]
        index = meta_all[s, picks:2 * picks, :]
        values = lax.fori_loop(
            0, table, lambda j, v: jnp.where(index == j, table_ref[j], v),
            jnp.zeros((picks, count), jnp.float32),
        )
        weights = route_scale * values / jnp.sum(values, axis=0, keepdims=True)
        for e in range(local):
            match = ids == c * local + e
            named = jnp.sum(jnp.where(match, 1.0, 0.0), axis=0, keepdims=True)
            weight = jnp.sum(jnp.where(match, weights, 0.0), axis=0, keepdims=True)
            wide = jnp.broadcast_to(named, (16, count)).astype(jnp.bfloat16)
            rank = jnp.dot(wide, before, preferred_element_type=jnp.float32)[0:1, :]
            rank = jnp.where(named > 0.5, rank, -1.0)
            chosen = jnp.where(line == rank, 1.0, 0.0)
            place[e, s] = chosen[:CAP].astype(jnp.bfloat16)
            spread[e, s] = chosen.T.astype(jnp.bfloat16)
            scale = jnp.sum(chosen[:CAP] * weight, axis=1, keepdims=True)
            slot_weight[e, s] = jnp.broadcast_to(scale, (CAP, 128))

    for d in range(1, rows + 1):
        for sign in (-1, 1):
            q = r + sign * d
            if d < rows:
                @pl.when((q >= 0) & (q < rows))
                def _():
                    tok_wait(0, q)
                    spread_tokens(q, has_up & (q < r), has_down & (q > r))

            p = r + sign * (d - 1)
            if d > 1 or sign < 0:
                @pl.when((p >= 0) & (p < rows))
                def _():
                    tok_wait(2, p)
                    tok_copy(4, p).start()
    for q in range(rows):
        tok_wait(1, q)
        tok_wait(3, q)

    def project(e):
        @pl.loop(0, chunks)
        def _(n):
            for copy in weight_copies(e, n):
                copy.wait()
            acc_gate[...] = jnp.zeros_like(acc_gate)
            acc_up[...] = jnp.zeros_like(acc_up)

            @pl.loop(0, rows)
            def _(j):
                depth = pl.ds(pl.multiple_of(j * width, width), width)
                x = tok_all[j]
                acc_gate[...] += jnp.dot(x, gate_buf[n, depth, :], preferred_element_type=jnp.float32)
                acc_up[...] += jnp.dot(x, up_buf[n, depth, :], preferred_element_type=jnp.float32)

            @pl.when(e + 1 < local)
            def _():
                for copy in weight_copies(e + 1, n):
                    copy.start()

            cut = pl.ds(pl.multiple_of(n * TILE, TILE), TILE)
            for s in range(cols):
                span = pl.ds(s * count, count)
                v = acc_gate[span, :]
                h = (v / (1.0 + jnp.exp(-v)) * acc_up[span, :]).astype(jnp.bfloat16)
                picked = jnp.dot(place[e, s], h, preferred_element_type=jnp.float32)
                hid[e, r, pl.ds(s * CAP, CAP), cut] = picked.astype(jnp.bfloat16)

        @pl.when(has_up)
        def _():
            hid_copy(0, e, r).start()

        @pl.when(has_down)
        def _():
            hid_copy(1, e, r).start()

    def forward(e, d):
        for sign in (-1, 1):
            q = r + sign * d

            @pl.when((q >= 0) & (q < rows))
            def _():
                view = hid.at[e, q]
                remote(view, view, hid_send.at[0, e, q], hid_recv.at[e, q], c, r).wait_recv()

                @pl.when(has_up if sign < 0 else has_down)
                def _():
                    hid_copy(0 if sign < 0 else 1, e, q).start()

    def finish(e):
        slot = e % 2
        down_copy(e, slot).wait()

        @pl.loop(0, width // TILE)
        def _(n):
            cut = pl.ds(pl.multiple_of(n * TILE, TILE), TILE)
            full = sum(
                jnp.dot(
                    hid[e, q], down_buf[slot, pl.ds(q * hidden, hidden), cut],
                    preferred_element_type=jnp.float32,
                )
                for q in range(rows)
            )
            for s in range(cols):
                scaled = full[s * CAP:(s + 1) * CAP] * slot_weight[e, s][:, 0:1]
                back = jnp.dot(
                    spread[e, s][:, :CAP], scaled.astype(jnp.bfloat16), preferred_element_type=jnp.float32
                )
                acc[pl.ds(s * count, count), cut] += back

        @pl.when(e + 2 < local)
        def _():
            down_copy(e + 2, slot).start()

    @pl.loop(0, local + rows - 1)
    def _(k):
        @pl.when(k < local)
        def _():
            project(k)

        for d in range(1, rows):
            @pl.when((k >= d) & (k - d < local))
            def _():
                forward(k - d, d)

        @pl.when(k >= rows - 1)
        def _():
            finish(k - (rows - 1))

    def mine(k):
        return acc[pl.ds(pl.multiple_of(col_of[k] * count, count), count), :]

    def part_copy(i):
        src = (part.at[0], part.at[1], x_out)[i]
        dst = (sib_in.at[0], sib_in.at[1], x_in)[i]
        return remote(src, dst, part_send.at[i], part_recv.at[i], col_of[2 if i == 2 else 1], r)

    part[0] = mine(3).astype(jnp.bfloat16)
    part_copy(0).start()
    part[1] = mine(1).astype(jnp.bfloat16)
    part_copy(1).start()
    part_copy(0).wait_recv()
    x_out[...] = (mine(2) + sib_in[0].astype(jnp.float32)).astype(jnp.bfloat16)
    part_copy(2).start()
    part_copy(1).wait_recv()
    part_copy(2).wait_recv()
    total = mine(0) + sib_in[1].astype(jnp.float32) + x_in[...].astype(jnp.float32)
    out_ref[...] = total.astype(out_ref.dtype)

    for i in range(3):
        part_copy(i).wait_send()
        meta_copy(i + 1).wait_send()
    for q in range(rows):
        for kind in range(5):
            if kind >= 2:
                tok_copy(kind, q).wait_send()
            else:
                @pl.when((has_up & (q <= r)) if kind == 0 else (has_down & (q >= r)))
                def _():
                    tok_copy(kind, q).wait_send()
                    for e in range(local):
                        hid_copy(kind, e, q).wait_send()


def scratch(geometry):
    cols, rows, count, picks, local, width, hidden, table = geometry
    slots, chunks = cols * CAP, hidden // TILE
    bf16, f32 = jnp.bfloat16, jnp.float32
    return [
        ((rows, cols * count, width), bf16),
        ((cols, 2 * picks, count), jnp.int32),
        ((chunks, rows * width, TILE), bf16),
        ((chunks, rows * width, TILE), bf16),
        ((2, rows * hidden, width), bf16),
        ((cols * count, TILE), f32),
        ((cols * count, TILE), f32),
        ((local, cols, CAP, count), bf16),
        ((local, cols, count, count), bf16),
        ((local, cols, CAP, 128), f32),
        ((local, rows, slots, hidden), bf16),
        ((cols * count, width), f32),
        ((2, count, width), bf16),
        ((2, count, width), bf16),
        ((count, width), bf16),
        ((count, width), bf16),
    ]


def kernel_shards(tokens, expert_ids, weight_index, combine_table, gate_weight, up_weight, down_weight):
    cols, rows = lax.axis_size("col"), lax.axis_size("row")
    count, picks = expert_ids.shape
    local, depth, hidden = gate_weight.shape
    geometry = (cols, rows, count, picks, local, tokens.shape[1], hidden, combine_table.shape[0])
    chunks = hidden // TILE
    meta = jnp.concatenate([expert_ids.T, weight_index.T], axis=0)
    dma = pltpu.SemaphoreType.DMA
    anywhere = pl.BlockSpec(memory_space=pl.ANY)
    slots = cols * CAP
    flops = 4 * cols * count * depth * hidden * local + 2 * slots * rows * hidden * tokens.shape[1] * local
    moved = 2 * (gate_weight.size + up_weight.size + down_weight.size)
    return pl.pallas_call(
        functools.partial(expert_kernel, geometry),
        out_shape=jax.ShapeDtypeStruct(tokens.shape, jnp.bfloat16),
        in_specs=[
            anywhere,
            pl.BlockSpec(memory_space=pltpu.VMEM),
            pl.BlockSpec(memory_space=pltpu.SMEM),
            anywhere, anywhere, anywhere,
        ],
        out_specs=pl.BlockSpec(memory_space=pltpu.VMEM),
        scratch_shapes=[pltpu.VMEM(shape, kind) for shape, kind in scratch(geometry)] + [
            dma, dma((chunks,)), dma((chunks,)), dma((2,)),
            dma((3,)), dma((3,)), dma((5, rows)), dma((4, rows)),
            dma((2, local, rows)), dma((local, rows)), dma((3,)), dma((3,)),
        ],
        compiler_params=pltpu.CompilerParams(
            collective_id=0, has_side_effects=True, vmem_limit_bytes=VMEM_BYTES
        ),
        cost_estimate=pl.CostEstimate(flops=flops, bytes_accessed=moved, transcendentals=0),
    )(tokens, meta, combine_table, gate_weight, up_weight, down_weight)


def shards(tokens, expert_ids, weight_index, combine_table, gate_weight, up_weight, down_weight):
    cols, rows = lax.axis_size("col"), lax.axis_size("row")
    count, picks = expert_ids.shape
    local, depth, hidden = gate_weight.shape
    width = tokens.shape[1]
    geometry = (cols, rows, count, picks, local, width, hidden, combine_table.shape[0])
    held = sum(jnp.dtype(kind).itemsize * functools.reduce(lambda a, b: a * b, shape) for shape, kind in scratch(geometry))
    fits = cols == 4 and hidden % TILE == 0 and width % TILE == 0 and count % 128 == 0 and held < VMEM_BYTES * 9 // 10
    form = kernel_shards if fits else plain_shards
    return form(tokens, expert_ids, weight_index, combine_table, gate_weight, up_weight, down_weight)


def solution(mesh):
    in_specs = (
        P(("grp", "col"), "row"),
        P(("grp", "col"), None),
        P(("grp", "col"), None),
        P(),
        P("col", None, "row"),
        P("col", None, "row"),
        P("col", None, "row"),
    )
    out_specs = P(("grp", "col"), "row")
    return jax.shard_map(shards, mesh=mesh, in_specs=in_specs, out_specs=out_specs, check_vma=False)
```

```python
import functools

import jax
import jax.numpy as jnp
from jax import lax
from jax.experimental import pallas as pl
from jax.experimental.pallas import tpu as pltpu
from jax.sharding import PartitionSpec as P

CAP = 80


route_scale = 2.827


def slot_table(picked_ids, experts, capacity):
    count, picks = picked_ids.shape
    flat_ids = picked_ids.reshape(-1)
    one_hot = (flat_ids[:, None] == jnp.arange(experts, dtype=jnp.int32)[None, :]).astype(jnp.int32)
    ranking = jnp.sum((jnp.cumsum(one_hot, axis=0) - 1) * one_hot, axis=1)
    placing = flat_ids * capacity + ranking
    entries = jnp.arange(count * picks, dtype=jnp.int32) // picks
    holder = jnp.full((experts * capacity,), -1, jnp.int32).at[placing].set(entries)
    return (holder, placing)


def combine_weights(weight_index, combine_table):
    table_size = combine_table.shape[0]
    match = weight_index[..., None] == jnp.arange(table_size, dtype=jnp.int32)
    table_values = jnp.sum(jnp.where(match, combine_table, jnp.float32(0.0)), axis=-1)
    return route_scale * table_values / jnp.sum(table_values, axis=-1, keepdims=True)


def select_rows(source, holder, col_count, local_experts):
    is_valid = holder >= 0
    picked = jnp.take(source, jnp.maximum(holder, 0), axis=0)
    picked = jnp.where(is_valid[:, None], picked, jnp.zeros((), source.dtype))
    return picked.reshape(col_count, local_experts, CAP, source.shape[1])


def plain_shards(tokens, expert_ids, weight_index, combine_table, gate_weight, up_weight, down_weight):
    col_count = lax.axis_size("col")
    local_experts = gate_weight.shape[0]
    experts = local_experts * col_count
    holder, placing = slot_table(expert_ids, experts, CAP)
    full_tokens = lax.all_gather(tokens, "row", axis=1, tiled=True)
    outgoing = select_rows(full_tokens, holder, col_count, local_experts)
    arrived = lax.all_to_all(outgoing, "col", split_axis=0, concat_axis=0, tiled=True)
    gate_part = jnp.einsum(
        "secw,ewf->secf", arrived, gate_weight, preferred_element_type=jnp.float32
    )
    up_part = jnp.einsum("secw,ewf->secf", arrived, up_weight, preferred_element_type=jnp.float32)
    hidden = (jax.nn.silu(gate_part) * up_part).astype(jnp.bfloat16)
    expert_out = jnp.einsum(
        "secf,efd->secd",
        lax.all_gather(hidden, "row", axis=3, tiled=True),
        down_weight,
        preferred_element_type=jnp.float32,
    ).astype(jnp.bfloat16)
    returned = lax.all_to_all(expert_out, "col", split_axis=0, concat_axis=0, tiled=True)
    features = returned.shape[3]
    gathered = jnp.take(returned.reshape(experts * CAP, features), placing, axis=0)
    gathered = gathered.reshape(expert_ids.shape + (features,)).astype(jnp.float32)
    weights = combine_weights(weight_index, combine_table)
    return jnp.sum(weights[..., None] * gathered, axis=1).astype(jnp.bfloat16)


TILE = 256
VMEM_BYTES = 60 * 1024 * 1024
MESH = pl.DeviceIdType.MESH


def expert_kernel(
    geometry, tok_hbm, meta_ref, table_ref, gate_hbm, up_hbm, down_hbm, out_ref,
    tok_all, meta_all, gate_buf, up_buf, down_buf, acc_gate, acc_up, place, spread, slot_weight,
    hid, acc, part, sib_in, x_out, x_in,
    local_sem, gate_sem, up_sem, down_sem, meta_send, meta_recv, tok_send, tok_recv,
    hid_send, hid_recv, part_send, part_recv,
):
    cols, rows, count, picks, local, width, hidden, table = geometry
    slots = cols * CAP // 2
    chunks = hidden // TILE
    units = 2 * local
    g = lax.axis_index("grp")
    c = lax.axis_index("col")
    r = lax.axis_index("row")
    core, chip = c % 2, c // 2
    col_of = [c, 2 * chip + 1 - core, 2 * (1 - chip) + core, 2 * (1 - chip) + 1 - core]
    has_up, has_down = r < rows - 1, r > 0

    def remote(src, dst, send, recv, col, row):
        return pltpu.make_async_remote_copy(
            src_ref=src, dst_ref=dst, send_sem=send, recv_sem=recv,
            device_id=(g, col, row), device_id_type=MESH,
        )

    def block(q, s):
        return tok_all.at[q, pl.ds(pl.multiple_of(s * count, count), count), :]

    def tok_copy(kind, q):
        s = col_of[2] if kind == 4 else c
        col = (c, c, col_of[1], col_of[2], col_of[1])[kind]
        row = (r + 1, r - 1, r, r, r)[kind]
        relation = (0, 0, 1, 2, 3)[kind]
        return remote(block(q, s), block(q, s), tok_send.at[kind, q], tok_recv.at[relation, q], col, row)

    def tok_wait(relation, q):
        view = block(q, col_of[relation])
        remote(view, view, tok_send.at[0, q], tok_recv.at[relation, q], c, r).wait_recv()

    def hid_copy(direction, e, q):
        view = hid.at[e, q]
        return remote(
            view, view, hid_send.at[direction, e, q], hid_recv.at[e, q], c, (r + 1, r - 1)[direction]
        )

    def weight_copies(e, n):
        cut = pl.ds(pl.multiple_of(n * TILE, TILE), TILE)
        return (
            pltpu.make_async_copy(gate_hbm.at[e, :, cut], gate_buf.at[n], gate_sem.at[n]),
            pltpu.make_async_copy(up_hbm.at[e, :, cut], up_buf.at[n], up_sem.at[n]),
        )

    def down_copy(e, slot):
        return pltpu.make_async_copy(down_hbm.at[e], down_buf.at[slot], down_sem.at[slot])

    local_copy = pltpu.make_async_copy(tok_hbm, block(r, c), local_sem)
    local_copy.start()
    for n in range(chunks):
        for copy in weight_copies(0, n):
            copy.start()
    for e in range(min(2, local)):
        down_copy(e, e).start()

    barrier = pltpu.get_barrier_semaphore()
    for k in (1, 2, 3):
        pl.semaphore_signal(barrier, inc=1, device_id=(g, col_of[k], r), device_id_type=MESH)

    @pl.when(has_up)
    def _():
        pl.semaphore_signal(barrier, inc=1, device_id=(g, c, r + 1), device_id_type=MESH)

    @pl.when(has_down)
    def _():
        pl.semaphore_signal(barrier, inc=1, device_id=(g, c, r - 1), device_id_type=MESH)

    pl.semaphore_wait(barrier, 3 + jnp.where(has_up, 1, 0) + jnp.where(has_down, 1, 0))

    def meta_copy(k):
        return remote(meta_ref, meta_all.at[c], meta_send.at[k - 1], meta_recv.at[k - 1], col_of[k], r)

    for k in (1, 2, 3):
        meta_copy(k).start()
    local_copy.wait()

    def spread_tokens(q, upward, downward):
        @pl.when(upward)
        def _():
            tok_copy(0, q).start()

        @pl.when(downward)
        def _():
            tok_copy(1, q).start()

        tok_copy(3, q).start()
        tok_copy(2, q).start()

    spread_tokens(r, has_up, has_down)

    meta_all[c] = meta_ref[...]
    acc[...] = jnp.zeros_like(acc)
    for k in (1, 2, 3):
        view = meta_all.at[col_of[k]]
        remote(meta_ref, view, meta_send.at[k - 1], meta_recv.at[k - 1], c, r).wait_recv()
    before = (
        lax.broadcasted_iota(jnp.int32, (count, count), 0)
        < lax.broadcasted_iota(jnp.int32, (count, count), 1)
    ).astype(jnp.float32).astype(jnp.bfloat16)
    line = lax.broadcasted_iota(jnp.int32, (count, count), 0).astype(jnp.float32)

    @pl.loop(0, cols)
    def _(s):
        ids = meta_all[s, 0:picks, :]
        index = meta_all[s, picks:2 * picks, :]
        values = lax.fori_loop(
            0, table, lambda j, v: jnp.where(index == j, table_ref[j], v),
            jnp.zeros((picks, count), jnp.float32),
        )
        weights = route_scale * values / jnp.sum(values, axis=0, keepdims=True)
        for e in range(local):
            match = ids == c * local + e
            named = jnp.sum(jnp.where(match, 1.0, 0.0), axis=0, keepdims=True)
            weight = jnp.sum(jnp.where(match, weights, 0.0), axis=0, keepdims=True)
            wide = jnp.broadcast_to(named, (16, count)).astype(jnp.bfloat16)
            rank = jnp.dot(wide, before, preferred_element_type=jnp.float32)[0:1, :]
            rank = jnp.where(named > 0.5, rank, -1.0)
            chosen = jnp.where(line == rank, 1.0, 0.0)
            place[e, s] = chosen[:CAP].astype(jnp.bfloat16)
            spread[e, s] = chosen.T.astype(jnp.bfloat16)
            scale = jnp.sum(chosen[:CAP] * weight, axis=1, keepdims=True)
            slot_weight[e, s] = jnp.broadcast_to(scale, (CAP, 128))

    for d in range(1, rows):
        for sign in (-1, 1):
            q = r + sign * d

            @pl.when((q >= 0) & (q < rows))
            def _():
                tok_wait(0, q)
                spread_tokens(q, has_up & (q < r), has_down & (q > r))
    for q in range(rows):
        tok_wait(1, q)

    def pass_on(d):
        for sign in (-1, 1) if d > 0 else (1,):
            q = r + sign * d

            @pl.when((q >= 0) & (q < rows))
            def _():
                tok_wait(2, q)
                tok_copy(4, q).start()

    def chip_of(u):
        own = (u == 0) | ((u >= 2) & (u % 2 == 1))
        return jnp.where(own, chip, 1 - chip)

    def project(u):
        e, h = u // 2, u % 2
        first = 2 * chip_of(u)
        span = pl.ds(pl.multiple_of(first * count, 2 * count), 2 * count)

        @pl.loop(0, chunks)
        def _(n):
            @pl.when(h == 0)
            def _():
                for copy in weight_copies(e, n):
                    copy.wait()

            acc_gate[...] = jnp.zeros_like(acc_gate)
            acc_up[...] = jnp.zeros_like(acc_up)

            @pl.loop(0, rows)
            def _(j):
                depth = pl.ds(pl.multiple_of(j * width, width), width)
                x = tok_all[j, span, :]
                acc_gate[...] += jnp.dot(x, gate_buf[n, depth, :], preferred_element_type=jnp.float32)
                acc_up[...] += jnp.dot(x, up_buf[n, depth, :], preferred_element_type=jnp.float32)

            @pl.when((h == 1) & (e + 1 < local))
            def _():
                for copy in weight_copies(e + 1, n):
                    copy.start()

            cut = pl.ds(pl.multiple_of(n * TILE, TILE), TILE)
            for i in range(2):
                lines = pl.ds(i * count, count)
                v = acc_gate[lines, :]
                hv = (v / (1.0 + jnp.exp(-v)) * acc_up[lines, :]).astype(jnp.bfloat16)
                picked = jnp.dot(place[e, first + i], hv, preferred_element_type=jnp.float32)
                hid[u, r, pl.ds(i * CAP, CAP), cut] = picked.astype(jnp.bfloat16)

        @pl.when(has_up)
        def _():
            hid_copy(0, u, r).start()

        @pl.when(has_down)
        def _():
            hid_copy(1, u, r).start()

    def forward(u, d):
        for sign in (-1, 1):
            q = r + sign * d

            @pl.when((q >= 0) & (q < rows))
            def _():
                view = hid.at[u, q]
                remote(view, view, hid_send.at[0, u, q], hid_recv.at[u, q], c, r).wait_recv()

                @pl.when(has_up if sign < 0 else has_down)
                def _():
                    hid_copy(0 if sign < 0 else 1, u, q).start()

    def finish(u):
        e, h = u // 2, u % 2
        first = 2 * chip_of(u)
        slot = e % 2

        @pl.when(h == 0)
        def _():
            down_copy(e, slot).wait()

        @pl.loop(0, width // TILE)
        def _(n):
            cut = pl.ds(pl.multiple_of(n * TILE, TILE), TILE)
            full = sum(
                jnp.dot(
                    hid[u, q], down_buf[slot, pl.ds(q * hidden, hidden), cut],
                    preferred_element_type=jnp.float32,
                )
                for q in range(rows)
            )
            for i in range(2):
                scale = slot_weight[e, first + i]
                scaled = full[i * CAP:(i + 1) * CAP] * jnp.concatenate([scale] * (TILE // 128), axis=1)
                back = jnp.dot(
                    spread[e, first + i][:, :CAP], scaled.astype(jnp.bfloat16),
                    preferred_element_type=jnp.float32,
                )
                lines = pl.ds(pl.multiple_of((first + i) * count, count), count)
                acc[lines, cut] += back

        @pl.when((h == 1) & (e + 2 < local))
        def _():
            down_copy(e + 2, slot).start()

    def mine(k):
        return acc[pl.ds(pl.multiple_of(col_of[k] * count, count), count), :]

    def part_copy(i):
        src = (part.at[0], part.at[1], x_out)[i]
        dst = (sib_in.at[0], sib_in.at[1], x_in)[i]
        return remote(src, dst, part_send.at[i], part_recv.at[i], col_of[2 if i == 2 else 1], r)

    last = units + rows - 2

    @pl.loop(0, last + 1)
    def _(k):
        @pl.when(k == 1)
        def _():
            pass_on(0)
            for d in range(1, rows):
                pass_on(d)
                if d < rows - 1:
                    forward(0, d)
            for q in range(rows):
                tok_wait(3, q)

        @pl.when(k < units)
        def _():
            project(k)

        @pl.when(k == last)
        def _():
            part[0] = mine(3).astype(jnp.bfloat16)
            part_copy(0).start()
            part_copy(0).wait_recv()
            x_out[...] = (mine(2) + sib_in[0].astype(jnp.float32)).astype(jnp.bfloat16)
            part_copy(2).start()

        for d in range(1, rows):
            least = 0 if d == rows - 1 else 1

            @pl.when((k >= d + least) & (k - d < units))
            def _():
                forward(k - d, d)

        @pl.when(k >= rows - 1)
        def _():
            finish(k - (rows - 1))

    part[1] = mine(1).astype(jnp.bfloat16)
    part_copy(1).start()
    part_copy(1).wait_recv()
    part_copy(2).wait_recv()
    total = mine(0) + sib_in[1].astype(jnp.float32) + x_in[...].astype(jnp.float32)
    out_ref[...] = total.astype(out_ref.dtype)

    for i in range(3):
        part_copy(i).wait_send()
        meta_copy(i + 1).wait_send()
    for q in range(rows):
        for kind in range(5):
            if kind >= 2:
                tok_copy(kind, q).wait_send()
            else:
                @pl.when((has_up & (q <= r)) if kind == 0 else (has_down & (q >= r)))
                def _():
                    tok_copy(kind, q).wait_send()
                    for u in range(units):
                        hid_copy(kind, u, q).wait_send()


def scratch(geometry):
    cols, rows, count, picks, local, width, hidden, table = geometry
    slots, chunks = cols * CAP // 2, hidden // TILE
    bf16, f32 = jnp.bfloat16, jnp.float32
    return [
        ((rows, cols * count, width), bf16),
        ((cols, 2 * picks, count), jnp.int32),
        ((chunks, rows * width, TILE), bf16),
        ((chunks, rows * width, TILE), bf16),
        ((2, rows * hidden, width), bf16),
        ((2 * count, TILE), f32),
        ((2 * count, TILE), f32),
        ((local, cols, CAP, count), bf16),
        ((local, cols, count, count), bf16),
        ((local, cols, CAP, 128), f32),
        ((2 * local, rows, slots, hidden), bf16),
        ((cols * count, width), f32),
        ((2, count, width), bf16),
        ((2, count, width), bf16),
        ((count, width), bf16),
        ((count, width), bf16),
    ]


def kernel_shards(tokens, expert_ids, weight_index, combine_table, gate_weight, up_weight, down_weight):
    cols, rows = lax.axis_size("col"), lax.axis_size("row")
    count, picks = expert_ids.shape
    local, depth, hidden = gate_weight.shape
    geometry = (cols, rows, count, picks, local, tokens.shape[1], hidden, combine_table.shape[0])
    chunks = hidden // TILE
    meta = jnp.concatenate([expert_ids.T, weight_index.T], axis=0)
    dma = pltpu.SemaphoreType.DMA
    anywhere = pl.BlockSpec(memory_space=pl.ANY)
    slots = cols * CAP
    flops = 4 * cols * count * depth * hidden * local + 2 * slots * rows * hidden * tokens.shape[1] * local
    moved = 2 * (gate_weight.size + up_weight.size + down_weight.size)
    return pl.pallas_call(
        functools.partial(expert_kernel, geometry),
        out_shape=jax.ShapeDtypeStruct(tokens.shape, jnp.bfloat16),
        in_specs=[
            anywhere,
            pl.BlockSpec(memory_space=pltpu.VMEM),
            pl.BlockSpec(memory_space=pltpu.SMEM),
            anywhere, anywhere, anywhere,
        ],
        out_specs=pl.BlockSpec(memory_space=pltpu.VMEM),
        scratch_shapes=[pltpu.VMEM(shape, kind) for shape, kind in scratch(geometry)] + [
            dma, dma((chunks,)), dma((chunks,)), dma((2,)),
            dma((3,)), dma((3,)), dma((5, rows)), dma((4, rows)),
            dma((2, 2 * local, rows)), dma((2 * local, rows)), dma((3,)), dma((3,)),
        ],
        compiler_params=pltpu.CompilerParams(
            collective_id=0, has_side_effects=True, vmem_limit_bytes=VMEM_BYTES
        ),
        cost_estimate=pl.CostEstimate(flops=flops, bytes_accessed=moved, transcendentals=0),
    )(tokens, meta, combine_table, gate_weight, up_weight, down_weight)


def shards(tokens, expert_ids, weight_index, combine_table, gate_weight, up_weight, down_weight):
    cols, rows = lax.axis_size("col"), lax.axis_size("row")
    count, picks = expert_ids.shape
    local, depth, hidden = gate_weight.shape
    width = tokens.shape[1]
    geometry = (cols, rows, count, picks, local, width, hidden, combine_table.shape[0])
    held = sum(jnp.dtype(kind).itemsize * functools.reduce(lambda a, b: a * b, shape) for shape, kind in scratch(geometry))
    fits = cols == 4 and rows > 1 and local > 1 and CAP % 16 == 0 and hidden % TILE == 0 and width % TILE == 0 and count % 128 == 0 and held < VMEM_BYTES * 9 // 10
    form = kernel_shards if fits else plain_shards
    return form(tokens, expert_ids, weight_index, combine_table, gate_weight, up_weight, down_weight)


def solution(mesh):
    in_specs = (
        P(("grp", "col"), "row"),
        P(("grp", "col"), None),
        P(("grp", "col"), None),
        P(),
        P("col", None, "row"),
        P("col", None, "row"),
        P("col", None, "row"),
    )
    out_specs = P(("grp", "col"), "row")
    return jax.shard_map(shards, mesh=mesh, in_specs=in_specs, out_specs=out_specs, check_vma=False)
```

```python
import functools

import jax
import jax.numpy as jnp
from jax import lax
from jax.experimental import pallas as pl
from jax.experimental.pallas import tpu as pltpu
from jax.sharding import PartitionSpec as P

CAP = 80


route_scale = 2.827


def slot_table(picked_ids, experts, capacity):
    count, picks = picked_ids.shape
    flat_ids = picked_ids.reshape(-1)
    one_hot = (flat_ids[:, None] == jnp.arange(experts, dtype=jnp.int32)[None, :]).astype(jnp.int32)
    ranking = jnp.sum((jnp.cumsum(one_hot, axis=0) - 1) * one_hot, axis=1)
    placing = flat_ids * capacity + ranking
    entries = jnp.arange(count * picks, dtype=jnp.int32) // picks
    holder = jnp.full((experts * capacity,), -1, jnp.int32).at[placing].set(entries)
    return (holder, placing)


def combine_weights(weight_index, combine_table):
    table_size = combine_table.shape[0]
    match = weight_index[..., None] == jnp.arange(table_size, dtype=jnp.int32)
    table_values = jnp.sum(jnp.where(match, combine_table, jnp.float32(0.0)), axis=-1)
    return route_scale * table_values / jnp.sum(table_values, axis=-1, keepdims=True)


def select_rows(source, holder, col_count, local_experts):
    is_valid = holder >= 0
    picked = jnp.take(source, jnp.maximum(holder, 0), axis=0)
    picked = jnp.where(is_valid[:, None], picked, jnp.zeros((), source.dtype))
    return picked.reshape(col_count, local_experts, CAP, source.shape[1])


def plain_shards(tokens, expert_ids, weight_index, combine_table, gate_weight, up_weight, down_weight):
    col_count = lax.axis_size("col")
    local_experts = gate_weight.shape[0]
    experts = local_experts * col_count
    holder, placing = slot_table(expert_ids, experts, CAP)
    full_tokens = lax.all_gather(tokens, "row", axis=1, tiled=True)
    outgoing = select_rows(full_tokens, holder, col_count, local_experts)
    arrived = lax.all_to_all(outgoing, "col", split_axis=0, concat_axis=0, tiled=True)
    gate_part = jnp.einsum(
        "secw,ewf->secf", arrived, gate_weight, preferred_element_type=jnp.float32
    )
    up_part = jnp.einsum("secw,ewf->secf", arrived, up_weight, preferred_element_type=jnp.float32)
    hidden = (jax.nn.silu(gate_part) * up_part).astype(jnp.bfloat16)
    expert_out = jnp.einsum(
        "secf,efd->secd",
        lax.all_gather(hidden, "row", axis=3, tiled=True),
        down_weight,
        preferred_element_type=jnp.float32,
    ).astype(jnp.bfloat16)
    returned = lax.all_to_all(expert_out, "col", split_axis=0, concat_axis=0, tiled=True)
    features = returned.shape[3]
    gathered = jnp.take(returned.reshape(experts * CAP, features), placing, axis=0)
    gathered = gathered.reshape(expert_ids.shape + (features,)).astype(jnp.float32)
    weights = combine_weights(weight_index, combine_table)
    return jnp.sum(weights[..., None] * gathered, axis=1).astype(jnp.bfloat16)


TILE = 256
VMEM_BYTES = 60 * 1024 * 1024
MESH = pl.DeviceIdType.MESH


def expert_kernel(
    geometry, tok_hbm, meta_ref, table_ref, gate_hbm, up_hbm, down_hbm, out_ref,
    tok_all, meta_all, gate_buf, up_buf, down_buf, acc_gate, acc_up, place, spread, slot_weight,
    hid, acc, part, sib_in, x_out, x_in,
    local_sem, gate_sem, up_sem, down_sem, meta_send, meta_recv, tok_send, tok_recv,
    hid_send, hid_recv, part_send, part_recv,
):
    cols, rows, count, picks, local, width, hidden, table = geometry
    slots = cols * CAP // 2
    chunks = hidden // TILE
    units = 2 * local
    g = lax.axis_index("grp")
    c = lax.axis_index("col")
    r = lax.axis_index("row")
    core, chip = c % 2, c // 2
    col_of = [c, 2 * chip + 1 - core, 2 * (1 - chip) + core, 2 * (1 - chip) + 1 - core]
    has_up, has_down = r < rows - 1, r > 0

    def remote(src, dst, send, recv, col, row):
        return pltpu.make_async_remote_copy(
            src_ref=src, dst_ref=dst, send_sem=send, recv_sem=recv,
            device_id=(g, col, row), device_id_type=MESH,
        )

    def block(q, s):
        return tok_all.at[q, pl.ds(pl.multiple_of(s * count, count), count), :]

    def tok_copy(kind, q):
        s = col_of[2] if kind == 4 else c
        col = (c, c, col_of[1], col_of[2], col_of[1])[kind]
        row = (r + 1, r - 1, r, r, r)[kind]
        relation = (0, 0, 1, 2, 3)[kind]
        return remote(block(q, s), block(q, s), tok_send.at[kind, q], tok_recv.at[relation, q], col, row)

    def tok_wait(relation, q):
        view = block(q, col_of[relation])
        remote(view, view, tok_send.at[0, q], tok_recv.at[relation, q], c, r).wait_recv()

    def hid_copy(direction, e, q):
        view = hid.at[e, q]
        return remote(
            view, view, hid_send.at[direction, e, q], hid_recv.at[e, q], c, (r + 1, r - 1)[direction]
        )

    def weight_copies(e, n):
        cut = pl.ds(pl.multiple_of(n * TILE, TILE), TILE)
        return (
            pltpu.make_async_copy(gate_hbm.at[e, :, cut], gate_buf.at[n], gate_sem.at[n]),
            pltpu.make_async_copy(up_hbm.at[e, :, cut], up_buf.at[n], up_sem.at[n]),
        )

    def down_copy(e, slot):
        return pltpu.make_async_copy(down_hbm.at[e], down_buf.at[slot], down_sem.at[slot])

    local_copy = pltpu.make_async_copy(tok_hbm, block(r, c), local_sem)
    local_copy.start()
    for n in range(chunks):
        for copy in weight_copies(0, n):
            copy.start()
    for e in range(min(2, local)):
        down_copy(e, e).start()

    barrier = pltpu.get_barrier_semaphore()
    for k in (1, 2, 3):
        pl.semaphore_signal(barrier, inc=1, device_id=(g, col_of[k], r), device_id_type=MESH)

    @pl.when(has_up)
    def _():
        pl.semaphore_signal(barrier, inc=1, device_id=(g, c, r + 1), device_id_type=MESH)

    @pl.when(has_down)
    def _():
        pl.semaphore_signal(barrier, inc=1, device_id=(g, c, r - 1), device_id_type=MESH)

    pl.semaphore_wait(barrier, 3 + jnp.where(has_up, 1, 0) + jnp.where(has_down, 1, 0))

    def meta_copy(k):
        return remote(meta_ref, meta_all.at[c], meta_send.at[k - 1], meta_recv.at[k - 1], col_of[k], r)

    for k in (1, 2, 3):
        meta_copy(k).start()
    local_copy.wait()

    def spread_tokens(q, upward, downward):
        @pl.when(upward)
        def _():
            tok_copy(0, q).start()

        @pl.when(downward)
        def _():
            tok_copy(1, q).start()

        tok_copy(3, q).start()
        tok_copy(2, q).start()

    spread_tokens(r, has_up, has_down)

    meta_all[c] = meta_ref[...]
    acc[...] = jnp.zeros_like(acc)
    for k in (1, 2, 3):
        view = meta_all.at[col_of[k]]
        remote(meta_ref, view, meta_send.at[k - 1], meta_recv.at[k - 1], c, r).wait_recv()
    before = (
        lax.broadcasted_iota(jnp.int32, (count, count), 0)
        < lax.broadcasted_iota(jnp.int32, (count, count), 1)
    ).astype(jnp.float32).astype(jnp.bfloat16)
    line = lax.broadcasted_iota(jnp.int32, (count, count), 0).astype(jnp.float32)

    @pl.loop(0, cols)
    def _(s):
        ids = meta_all[s, 0:picks, :]
        index = meta_all[s, picks:2 * picks, :]
        values = lax.fori_loop(
            0, table, lambda j, v: jnp.where(index == j, table_ref[j], v),
            jnp.zeros((picks, count), jnp.float32),
        )
        weights = route_scale * values / jnp.sum(values, axis=0, keepdims=True)
        for e in range(local):
            match = ids == c * local + e
            named = jnp.sum(jnp.where(match, 1.0, 0.0), axis=0, keepdims=True)
            weight = jnp.sum(jnp.where(match, weights, 0.0), axis=0, keepdims=True)
            wide = jnp.broadcast_to(named, (16, count)).astype(jnp.bfloat16)
            rank = jnp.dot(wide, before, preferred_element_type=jnp.float32)[0:1, :]
            rank = jnp.where(named > 0.5, rank, -1.0)
            chosen = jnp.where(line == rank, 1.0, 0.0)
            place[e, s] = chosen[:CAP].astype(jnp.bfloat16)
            spread[e, s] = chosen.T.astype(jnp.bfloat16)
            scale = jnp.sum(chosen[:CAP] * weight, axis=1, keepdims=True)
            slot_weight[e, s] = jnp.broadcast_to(scale, (CAP, 128))

    for d in range(1, rows):
        for sign in (-1, 1):
            q = r + sign * d

            @pl.when((q >= 0) & (q < rows))
            def _():
                tok_wait(0, q)
                spread_tokens(q, has_up & (q < r), has_down & (q > r))
    for q in range(rows):
        tok_wait(1, q)

    def pass_on(d):
        for sign in (-1, 1) if d > 0 else (1,):
            q = r + sign * d

            @pl.when((q >= 0) & (q < rows))
            def _():
                tok_wait(2, q)
                tok_copy(4, q).start()

    def chip_of(u):
        own = (u == 0) | ((u >= 2) & (u % 2 == 1))
        return jnp.where(own, chip, 1 - chip)

    def gate(e, s, v, up):
        h = (v / (1.0 + jnp.exp(-v)) * up).astype(jnp.bfloat16)
        return jnp.dot(place[e, s], h, preferred_element_type=jnp.float32).astype(jnp.bfloat16)

    def multiply(n, span, lines):
        acc_gate[lines, :] = jnp.zeros((lines.size, TILE), jnp.float32)
        acc_up[lines, :] = jnp.zeros((lines.size, TILE), jnp.float32)

        @pl.loop(0, rows)
        def _(j):
            depth = pl.ds(pl.multiple_of(j * width, width), width)
            x = tok_all[j, span, :]
            acc_gate[lines, :] += jnp.dot(x, gate_buf[n, depth, :], preferred_element_type=jnp.float32)
            acc_up[lines, :] += jnp.dot(x, up_buf[n, depth, :], preferred_element_type=jnp.float32)

    def fetch_next(e, n):
        @pl.when(e + 1 < local)
        def _():
            for copy in weight_copies(e + 1, n):
                copy.start()

    def send_own(u):
        @pl.when(has_up)
        def _():
            hid_copy(0, u, r).start()

        @pl.when(has_down)
        def _():
            hid_copy(1, u, r).start()

    def project_half(u):
        first = 2 * chip_of(u)
        span = pl.ds(pl.multiple_of(first * count, 2 * count), 2 * count)

        @pl.loop(0, chunks)
        def _(n):
            @pl.when(u == 0)
            def _():
                for copy in weight_copies(0, n):
                    copy.wait()

            multiply(n, span, pl.ds(0, 2 * count))

            @pl.when(u == 1)
            def _():
                fetch_next(0, n)

            cut = pl.ds(pl.multiple_of(n * TILE, TILE), TILE)
            for i in range(2):
                lines = pl.ds(i * count, count)
                hid[u, r, pl.ds(i * CAP, CAP), cut] = gate(0, first + i, acc_gate[lines, :], acc_up[lines, :])

        send_own(u)

    def project_whole(e):
        @pl.loop(0, chunks)
        def _(n):
            for copy in weight_copies(e, n):
                copy.wait()
            multiply(n, pl.ds(0, cols * count), pl.ds(0, cols * count))
            fetch_next(e, n)
            cut = pl.ds(pl.multiple_of(n * TILE, TILE), TILE)
            for s in range(cols):
                lines = pl.ds(s * count, count)
                u = 2 * e + jnp.where(chip == s // 2, 1, 0)
                hid[u, r, pl.ds((s % 2) * CAP, CAP), cut] = gate(e, s, acc_gate[lines, :], acc_up[lines, :])

        send_own(2 * e)
        send_own(2 * e + 1)

    def forward(u, d):
        for sign in (-1, 1):
            q = r + sign * d

            @pl.when((q >= 0) & (q < rows))
            def _():
                view = hid.at[u, q]
                remote(view, view, hid_send.at[0, u, q], hid_recv.at[u, q], c, r).wait_recv()

                @pl.when(has_up if sign < 0 else has_down)
                def _():
                    hid_copy(0 if sign < 0 else 1, u, q).start()

    def finish(u):
        e, h = u // 2, u % 2
        first = 2 * chip_of(u)
        slot = e % 2

        @pl.when(h == 0)
        def _():
            down_copy(e, slot).wait()

        @pl.loop(0, width // TILE)
        def _(n):
            cut = pl.ds(pl.multiple_of(n * TILE, TILE), TILE)
            full = sum(
                jnp.dot(
                    hid[u, q], down_buf[slot, pl.ds(q * hidden, hidden), cut],
                    preferred_element_type=jnp.float32,
                )
                for q in range(rows)
            )
            for i in range(2):
                scale = slot_weight[e, first + i]
                scaled = full[i * CAP:(i + 1) * CAP] * jnp.concatenate([scale] * (TILE // 128), axis=1)
                back = jnp.dot(
                    spread[e, first + i][:, :CAP], scaled.astype(jnp.bfloat16),
                    preferred_element_type=jnp.float32,
                )
                lines = pl.ds(pl.multiple_of((first + i) * count, count), count)
                acc[lines, cut] += back

        @pl.when((h == 1) & (e + 2 < local))
        def _():
            down_copy(e + 2, slot).start()

    def mine(k):
        return acc[pl.ds(pl.multiple_of(col_of[k] * count, count), count), :]

    def part_copy(i):
        src = (part.at[0], part.at[1], x_out)[i]
        dst = (sib_in.at[0], sib_in.at[1], x_in)[i]
        return remote(src, dst, part_send.at[i], part_recv.at[i], col_of[2 if i == 2 else 1], r)

    last = units + rows - 2

    @pl.loop(0, last + 1)
    def _(k):
        @pl.when(k == 1)
        def _():
            pass_on(0)
            for d in range(1, rows):
                pass_on(d)
                if d < rows - 1:
                    forward(0, d)
            for q in range(rows):
                tok_wait(3, q)

        @pl.when(k < 2)
        def _():
            project_half(k)

        @pl.when((k >= 2) & (k < units) & (k % 2 == 0))
        def _():
            project_whole(k // 2)

        @pl.when(k == last)
        def _():
            part[0] = mine(3).astype(jnp.bfloat16)
            part_copy(0).start()
            part_copy(0).wait_recv()
            x_out[...] = (mine(2) + sib_in[0].astype(jnp.float32)).astype(jnp.bfloat16)
            part_copy(2).start()

        for d in range(1, rows):
            least = 0 if d == rows - 1 else 1

            @pl.when((k >= d + least) & (k - d < units))
            def _():
                forward(k - d, d)

        @pl.when(k >= rows - 1)
        def _():
            finish(k - (rows - 1))

    part[1] = mine(1).astype(jnp.bfloat16)
    part_copy(1).start()
    part_copy(1).wait_recv()
    part_copy(2).wait_recv()
    total = mine(0) + sib_in[1].astype(jnp.float32) + x_in[...].astype(jnp.float32)
    out_ref[...] = total.astype(out_ref.dtype)

    for i in range(3):
        part_copy(i).wait_send()
        meta_copy(i + 1).wait_send()
    for q in range(rows):
        for kind in range(5):
            if kind >= 2:
                tok_copy(kind, q).wait_send()
            else:
                @pl.when((has_up & (q <= r)) if kind == 0 else (has_down & (q >= r)))
                def _():
                    tok_copy(kind, q).wait_send()
                    for u in range(units):
                        hid_copy(kind, u, q).wait_send()


def scratch(geometry):
    cols, rows, count, picks, local, width, hidden, table = geometry
    slots, chunks = cols * CAP // 2, hidden // TILE
    bf16, f32 = jnp.bfloat16, jnp.float32
    return [
        ((rows, cols * count, width), bf16),
        ((cols, 2 * picks, count), jnp.int32),
        ((chunks, rows * width, TILE), bf16),
        ((chunks, rows * width, TILE), bf16),
        ((2, rows * hidden, width), bf16),
        ((cols * count, TILE), f32),
        ((cols * count, TILE), f32),
        ((local, cols, CAP, count), bf16),
        ((local, cols, count, count), bf16),
        ((local, cols, CAP, 128), f32),
        ((2 * local, rows, slots, hidden), bf16),
        ((cols * count, width), f32),
        ((2, count, width), bf16),
        ((2, count, width), bf16),
        ((count, width), bf16),
        ((count, width), bf16),
    ]


def kernel_shards(tokens, expert_ids, weight_index, combine_table, gate_weight, up_weight, down_weight):
    cols, rows = lax.axis_size("col"), lax.axis_size("row")
    count, picks = expert_ids.shape
    local, depth, hidden = gate_weight.shape
    geometry = (cols, rows, count, picks, local, tokens.shape[1], hidden, combine_table.shape[0])
    chunks = hidden // TILE
    meta = jnp.concatenate([expert_ids.T, weight_index.T], axis=0)
    dma = pltpu.SemaphoreType.DMA
    anywhere = pl.BlockSpec(memory_space=pl.ANY)
    slots = cols * CAP
    flops = 4 * cols * count * depth * hidden * local + 2 * slots * rows * hidden * tokens.shape[1] * local
    moved = 2 * (gate_weight.size + up_weight.size + down_weight.size)
    return pl.pallas_call(
        functools.partial(expert_kernel, geometry),
        out_shape=jax.ShapeDtypeStruct(tokens.shape, jnp.bfloat16),
        in_specs=[
            anywhere,
            pl.BlockSpec(memory_space=pltpu.VMEM),
            pl.BlockSpec(memory_space=pltpu.SMEM),
            anywhere, anywhere, anywhere,
        ],
        out_specs=pl.BlockSpec(memory_space=pltpu.VMEM),
        scratch_shapes=[pltpu.VMEM(shape, kind) for shape, kind in scratch(geometry)] + [
            dma, dma((chunks,)), dma((chunks,)), dma((2,)),
            dma((3,)), dma((3,)), dma((5, rows)), dma((4, rows)),
            dma((2, 2 * local, rows)), dma((2 * local, rows)), dma((3,)), dma((3,)),
        ],
        compiler_params=pltpu.CompilerParams(
            collective_id=0, has_side_effects=True, vmem_limit_bytes=VMEM_BYTES
        ),
        cost_estimate=pl.CostEstimate(flops=flops, bytes_accessed=moved, transcendentals=0),
    )(tokens, meta, combine_table, gate_weight, up_weight, down_weight)


def shards(tokens, expert_ids, weight_index, combine_table, gate_weight, up_weight, down_weight):
    cols, rows = lax.axis_size("col"), lax.axis_size("row")
    count, picks = expert_ids.shape
    local, depth, hidden = gate_weight.shape
    width = tokens.shape[1]
    geometry = (cols, rows, count, picks, local, width, hidden, combine_table.shape[0])
    held = sum(jnp.dtype(kind).itemsize * functools.reduce(lambda a, b: a * b, shape) for shape, kind in scratch(geometry))
    fits = cols == 4 and rows > 1 and local > 1 and CAP % 16 == 0 and hidden % TILE == 0 and width % TILE == 0 and count % 128 == 0 and held < VMEM_BYTES * 9 // 10
    form = kernel_shards if fits else plain_shards
    return form(tokens, expert_ids, weight_index, combine_table, gate_weight, up_weight, down_weight)


def solution(mesh):
    in_specs = (
        P(("grp", "col"), "row"),
        P(("grp", "col"), None),
        P(("grp", "col"), None),
        P(),
        P("col", None, "row"),
        P("col", None, "row"),
        P("col", None, "row"),
    )
    out_specs = P(("grp", "col"), "row")
    return jax.shard_map(shards, mesh=mesh, in_specs=in_specs, out_specs=out_specs, check_vma=False)
```
